32 devices in a mesh: state: 4 (over x, core), snap: 8 (over z, y).
Axes of the slice: x: 2, y: 2, z: 4, core: 2. Of those that a mesh axis runs over, the one named last changes fastest.
Arguments:
- direct: float32 [2048, 1024], P('state', 'snap'), may hold values from -6 to 6
- adjoint: float32 [2048, 1024], P('state', 'snap'), may hold values from -6 to 6
- cell_weight: float32 [2048], P('state'), may hold values from 0.006629126 to 0.06629126
- right_vecs: float32 [1024, 256], P('snap'), may hold values from -0.1875 to 0.1875
- left_vecs: float32 [1024, 256], P('snap'), may hold values from -0.1875 to 0.1875
- inv_root: float32 [256], replicated, may hold values from 0.5 to 2
Outputs:
- gram: float32 [1024, 1024], P('state', 'snap')
- bal_modes: float32 [2048, 256], P(('state', 'snap'))
- adj_modes: float32 [2048, 256], P(('state', 'snap'))
The draws below stay inside these ranges and needn't reach their ends.
All inputs are finite; a program needn't handle non-finite values.
Results may differ from the reference program's by a relative error of at most 0.00013.
Values sent between devices are 32-bit elements; how exact they have to be, the bound alone decides.
A program may use at most 64 MiB of HBM per device.

```python
import math
import jax
import jax.numpy as jnp
from jax import lax

R = 256
NSTATE = 2048
MSNAP = 1024


def spiked(drawn, rng, source, target, shards_of, factor):
    def block_of(axis_at):
        return (jnp.arange(drawn.shape[axis_at]) // (drawn.shape[axis_at] // shards_of)).reshape((-1,) + (1,) * (drawn.ndim - 1 - axis_at))

    one_side = jax.random.permutation(rng, shards_of)[block_of(target)]
    second = (block_of(target) + shards_of // 2) % shards_of
    return jnp.where((block_of(source) == one_side) | (block_of(source) == second), factor * drawn, drawn)


def steps_of(key, extent, split, low, high):
    def one(axis_at, shards_of):
        steps = jax.random.uniform(jax.random.fold_in(jax.random.fold_in(key, 6), axis_at), (shards_of,), jnp.float32, low / len(split), high / len(split))
        return jnp.repeat(jnp.exp(steps), extent[axis_at] // shards_of).reshape((-1,) + (1,) * (len(extent) - axis_at - 1))

    factor_of = one(*split[0])
    for cut in split[1:]:
        factor_of = factor_of * one(*cut)
    return factor_of


def bell_draw(own_key, shape, spread, most, split=(), held_as=jnp.bfloat16):
    result = spread * jax.random.normal(own_key, shape, jnp.float32)
    if split:
        result = result * steps_of(own_key, shape, split, -0.22, 0.18)
    return jnp.clip(result, -most, most).astype(held_as)


def heavy_noise(rng, dims, spread, limit, pieces, heavy, kind=jnp.bfloat16):
    drawn = spread * jax.random.normal(rng, dims, jnp.float32)
    if pieces:
        drawn = drawn * steps_of(rng, dims, pieces, -0.22, 0.18)
    return jnp.clip(spiked(drawn, jax.random.fold_in(rng, 3), *heavy), -limit, limit).astype(kind)


def setup_inputs(seed: int = 0) -> dict:
    key_of = jax.random.split(jax.random.key(seed), 7)
    return {
        "direct": bell_draw(key_of[0], (NSTATE, MSNAP), 1.0, 6.0, ((0, 4), (1, 8)), jnp.float32),
        "adjoint": heavy_noise(key_of[1], (NSTATE, MSNAP), 1.0, 6.0, ((0, 4), (1, 8)), (0, 1, 8, 2.0), jnp.float32),
        "cell_weight": jnp.clip(jnp.exp(math.log(0.06629126) - 2.30258504 * jax.random.uniform(key_of[2], (NSTATE,), jnp.float32) ** steps_of(key_of[2], (NSTATE,), ((0, 4),), -0.2, 0.2)), 0.006629126, 0.06629126),
        "right_vecs": bell_draw(key_of[3], (MSNAP, R), MSNAP ** -0.5, 0.1875, ((0, 8),), jnp.float32),
        "left_vecs": bell_draw(key_of[4], (MSNAP, R), MSNAP ** -0.5, 0.1875, ((0, 8),), jnp.float32),
        "inv_root": jnp.clip(jnp.exp(jax.random.uniform(key_of[5], (R,), jnp.float32, math.log(0.5), math.log(2.0))), 0.5, 2.0),
    }


def reference(direct, adjoint, cell_weight, right_vecs, left_vecs, inv_root):
    weighted = adjoint * cell_weight[:, None]
    gram = jnp.dot(weighted.T, direct, precision=lax.Precision.HIGHEST, preferred_element_type=jnp.float32)
    bal_modes = jnp.dot(direct, right_vecs * inv_root[None, :], precision=lax.Precision.HIGHEST, preferred_element_type=jnp.float32)
    adj_modes = jnp.dot(adjoint, left_vecs * inv_root[None, :], precision=lax.Precision.HIGHEST, preferred_element_type=jnp.float32)
    return gram, bal_modes, adj_modes
```

```python
import functools
import math

import jax
import jax.numpy as jnp
from jax import lax
from jax.experimental import pallas as pl
from jax.experimental.pallas import tpu as pltpu
from jax.sharding import PartitionSpec as P

MESH = pl.DeviceIdType.MESH
F32 = jnp.float32
BF16 = jnp.bfloat16


def split(x):
    high = x.astype(BF16)
    return high, (x - high.astype(F32)).astype(BF16)


def product(a, b, side):
    def one(x, y):
        return lax.dot_general(x, y, (((side,), (0,)), ((), ())), preferred_element_type=F32)

    return one(a[0], b[0]) + (one(a[0], b[1]) + one(a[1], b[0]))


def kernel(far_count, near_count, chunks, a_ref, d_ref, w_ref, r_ref, l_ref, root_ref,
           gram_ref, bal_ref, adj_ref,
           a_held, d_held, r_held, wd_high, wd_low, g_out, g_in, part, part_out, part_in, m_out, m_in,
           a_send, a_recv, d_send, d_recv, r_send, r_recv, g_send, g_recv, p_send, p_recv, m_send, m_recv):
    state = lax.axis_index("state")
    snap = lax.axis_index("snap")
    far, near = snap // near_count, snap % near_count
    rows, width = a_ref.shape[2], a_ref.shape[3]
    cells = far_count * near_count * rows
    modes = r_ref.shape[1]
    slab = far_count // chunks

    def near_of(k):
        return lax.rem(near + k, near_count)

    def snap_of(far_at, near_at):
        return far_at * near_count + near_at

    barrier = pltpu.get_barrier_semaphore()

    def greet(k, carry):
        other = lax.rem(state + k // near_count, far_count)
        beside = lax.rem(near + k % near_count, near_count)
        pl.semaphore_signal(barrier, inc=1, device_id=(other, snap_of(far, beside)), device_id_type=MESH)
        return carry

    lax.fori_loop(1, far_count * near_count, greet, 0)

    def greet_far(k, carry):
        pl.semaphore_signal(barrier, inc=1, device_id=(state, snap_of(lax.rem(far + k, far_count), near)), device_id_type=MESH)
        return carry

    lax.fori_loop(1, far_count, greet_far, 0)
    pl.semaphore_wait(barrier, far_count * near_count - 1 + far_count - 1)

    def a_copy(way, step, chunk, src, block):
        go = 1 if way == 0 else -1
        at = pl.ds(chunk * slab, slab)
        return pltpu.make_async_remote_copy(
            src_ref=src.at[at],
            dst_ref=a_held.at[block, at],
            send_sem=a_send.at[way, step, chunk],
            recv_sem=a_recv.at[way, step, chunk],
            device_id=(state, snap_of(jnp.clip(far + go, 0, far_count - 1), near)),
            device_id_type=MESH,
        )

    has_next = (far < far_count - 1, far > 0)

    for chunk in range(chunks):
        for way in range(2):
            @pl.when(has_next[way])
            def _():
                a_copy(way, 0, chunk, a_ref, far).start()

    def d_copy(k):
        return pltpu.make_async_remote_copy(
            src_ref=d_ref, dst_ref=d_held.at[near], send_sem=d_send.at[k], recv_sem=d_recv.at[k],
            device_id=(state, snap_of(far, near_of(k))), device_id_type=MESH)

    def r_copy(k):
        return pltpu.make_async_remote_copy(
            src_ref=r_ref, dst_ref=r_held.at[near], send_sem=r_send.at[k], recv_sem=r_recv.at[k],
            device_id=(state, snap_of(far, near_of(k))), device_id_type=MESH)

    def p_copy(k):
        return pltpu.make_async_remote_copy(
            src_ref=part_out.at[k], dst_ref=part_in.at[k], send_sem=p_send.at[k], recv_sem=p_recv.at[k],
            device_id=(state, snap_of(far, near_of(k))), device_id_type=MESH)

    for k in range(1, near_count):
        d_copy(k).start()
        r_copy(k).start()

    root = root_ref[...]
    left = split(l_ref[...] * root)

    def adjoint_terms(near_at):
        x = a_ref[:, near_at].reshape(far_count * rows, width)
        return product(split(x), left, 1).reshape(far_count, rows, modes)

    for k in range(1, near_count):
        part_out[k] = adjoint_terms(near_of(k))
        p_copy(k).start()
    part[...] = adjoint_terms(near)

    def pass_on(step):
        for chunk in range(chunks):
            for way in range(2):
                block = far - step if way == 0 else far + step
                held = jnp.clip(block, 0, far_count - 1)

                @pl.when((block >= 0) & (block < far_count))
                def _():
                    a_copy(way, step - 1, chunk, a_ref, held).wait_recv()

                    @pl.when(has_next[way])
                    def _():
                        a_copy(way, step, chunk, a_held.at[held], held).start()

    def g_copy(block, beside):
        return pltpu.make_async_remote_copy(
            src_ref=g_out.at[block, beside], dst_ref=g_in.at[state, near],
            send_sem=g_send.at[block, beside], recv_sem=g_recv.at[state, near],
            device_id=(block, snap_of(far, beside)), device_id_type=MESH)

    def gram_block(value, block):
        x = split(value.reshape(cells, width))
        whole = product(x, (wd_high[...], wd_low[...]), 0)
        for beside in range(near_count):
            piece = whole[:, beside * width:(beside + 1) * width]
            own = (block == state) & (beside == near)

            @pl.when(own)
            def _():
                g_in[state, near] = piece

            @pl.when(jnp.logical_not(own))
            def _():
                g_out[block, beside] = piece
                g_copy(block, beside).start()

    def gram_step(step):
        for way in range(2):
            block = far - step if way == 0 else far + step
            held = jnp.clip(block, 0, far_count - 1)

            @pl.when((block >= 0) & (block < far_count))
            def _():
                gram_block(a_held[held], held)

    pass_on(1)

    for k in range(1, near_count):
        d_copy(k).wait_recv()
    d_held[near] = d_ref[...]
    weight = jnp.broadcast_to(w_ref[...], (width, cells)).T
    for beside in range(near_count):
        high, low = split(d_held[beside].reshape(cells, width) * weight)
        wd_high[:, beside * width:(beside + 1) * width] = high
        wd_low[:, beside * width:(beside + 1) * width] = low
    gram_block(a_ref[...], far)
    gram_step(1)
    if far_count > 2:
        pass_on(2)

    for k in range(1, near_count):
        r_copy(k).wait_recv()
    r_held[near] = r_ref[...]
    total = None
    for beside in range(near_count):
        x = d_held[beside, :, near].reshape(far_count * rows, width)
        term = product(split(x), split(r_held[beside] * root), 1)
        total = term if total is None else total + term
    m_out[:, 0] = total.reshape(far_count, rows, modes)
    total = part[...]
    for k in range(1, near_count):
        p_copy(k).wait_recv()
        total = total + part_in[k]
    m_out[:, 1] = total

    def m_copy(k):
        other = lax.rem(far + k, far_count)
        return pltpu.make_async_remote_copy(
            src_ref=m_out.at[other], dst_ref=m_in.at[k], send_sem=m_send.at[k], recv_sem=m_recv.at[k],
            device_id=(state, snap_of(other, near)), device_id_type=MESH)

    def each_far(first, body):
        def step(k, carry):
            body(k)
            return carry

        lax.fori_loop(first, far_count, step, 0)

    each_far(1, lambda k: m_copy(k).start())

    if far_count > 2:
        gram_step(2)

    def later(step):
        pass_on(step)
        gram_step(step)

    each_far(3, later)

    m_in[0] = m_out[far]
    each_far(1, lambda k: m_copy(k).wait_recv())
    bal_ref[...] = jnp.sum(m_in[:, 0], axis=0)
    adj_ref[...] = jnp.sum(m_in[:, 1], axis=0)

    def g_wait(k):
        source, beside = k // near_count, k % near_count

        @pl.when((source != state) | (beside != near))
        def _():
            pltpu.make_async_remote_copy(
                src_ref=g_out.at[source, beside], dst_ref=g_in.at[source, beside],
                send_sem=g_send.at[source, beside], recv_sem=g_recv.at[source, beside],
                device_id=(source, snap_of(far, beside)), device_id_type=MESH).wait_recv()

    lax.fori_loop(0, far_count * near_count, lambda k, c: (g_wait(k), c)[1], 0)
    for beside in range(near_count):
        gram_ref[beside] = jnp.sum(g_in[:, beside], axis=0)

    for k in range(1, near_count):
        d_copy(k).wait_send()
        r_copy(k).wait_send()
        p_copy(k).wait_send()
    each_far(1, lambda k: m_copy(k).wait_send())

    def g_left(k):
        block, beside = k // near_count, k % near_count

        @pl.when((block != state) | (beside != near))
        def _():
            g_copy(block, beside).wait_send()

    lax.fori_loop(0, far_count * near_count, lambda k, c: (g_left(k), c)[1], 0)

    def a_left(step):
        for chunk in range(chunks):
            for way in range(2):
                block = far - step if way == 0 else far + step

                @pl.when((block >= 0) & (block < far_count) & has_next[way])
                def _():
                    a_copy(way, step, chunk, a_ref, far).wait_send()

    each_far(0, a_left)


def local(direct, adjoint, cell_weight, right_vecs, left_vecs, inv_root):
    far_count = lax.axis_size("state")
    near_count = lax.axis_size("snap") // far_count
    cells, width = direct.shape
    modes = right_vecs.shape[1]
    rows = cells // (far_count * near_count)
    chunks = math.gcd(far_count, 4)
    block = (far_count, near_count, rows, width)
    vmem = pl.BlockSpec(memory_space=pltpu.VMEM)
    dma = pltpu.SemaphoreType.DMA
    gram, bal, adj = pl.pallas_call(
        functools.partial(kernel, far_count, near_count, chunks),
        out_shape=(
            jax.ShapeDtypeStruct((near_count, width, width), F32),
            jax.ShapeDtypeStruct((rows, modes), F32),
            jax.ShapeDtypeStruct((rows, modes), F32),
        ),
        in_specs=[vmem] * 6,
        out_specs=(vmem,) * 3,
        scratch_shapes=[
            pltpu.VMEM((far_count,) + block, F32),
            pltpu.VMEM((near_count,) + block, F32),
            pltpu.VMEM((near_count, width, modes), F32),
            pltpu.VMEM((cells, near_count * width), BF16),
            pltpu.VMEM((cells, near_count * width), BF16),
            pltpu.VMEM((far_count, near_count, width, width), F32),
            pltpu.VMEM((far_count, near_count, width, width), F32),
            pltpu.VMEM((far_count, rows, modes), F32),
            pltpu.VMEM((near_count, far_count, rows, modes), F32),
            pltpu.VMEM((near_count, far_count, rows, modes), F32),
            pltpu.VMEM((far_count, 2, rows, modes), F32),
            pltpu.VMEM((far_count, 2, rows, modes), F32),
            dma((2, far_count, chunks)),
            dma((2, far_count, chunks)),
            dma((near_count,)),
            dma((near_count,)),
            dma((near_count,)),
            dma((near_count,)),
            dma((far_count, near_count)),
            dma((far_count, near_count)),
            dma((near_count,)),
            dma((near_count,)),
            dma((far_count,)),
            dma((far_count,)),
        ],
        compiler_params=pltpu.CompilerParams(
            collective_id=0, has_side_effects=True, vmem_limit_bytes=48 * 1024 * 1024
        ),
    )(
        adjoint.reshape(block),
        direct.reshape(block),
        cell_weight.reshape(1, cells),
        right_vecs,
        left_vecs,
        inv_root.reshape(1, modes),
    )
    return gram.reshape(near_count * width, width), bal, adj


def solution(mesh):
    in_specs = (
        P("state", "snap"),
        P("state", "snap"),
        P("state"),
        P("snap", None),
        P("snap", None),
        P(),
    )
    out_specs = (P("state", "snap"), P(("state", "snap"), None), P(("state", "snap"), None))
    return jax.shard_map(local, mesh=mesh, in_specs=in_specs, out_specs=out_specs, check_vma=False)
```

```python
import functools
import math

import jax
import jax.numpy as jnp
from jax import lax
from jax.experimental import pallas as pl
from jax.experimental.pallas import tpu as pltpu
from jax.sharding import PartitionSpec as P

MESH = pl.DeviceIdType.MESH
F32 = jnp.float32
BF16 = jnp.bfloat16


def split(x):
    high = x.astype(BF16)
    return high, (x - high.astype(F32)).astype(BF16)


def product(a, b, side):
    def one(x, y):
        return lax.dot_general(x, y, (((side,), (0,)), ((), ())), preferred_element_type=F32)

    return one(a[0], b[0]) + (one(a[0], b[1]) + one(a[1], b[0]))


def kernel(far_count, near_count, chunks, a_hbm, d_hbm, w_hbm, r_hbm, l_hbm, root_hbm,
           gram_ref, bal_ref, adj_ref, a_ref, l_ref, w_ref, root_ref, load_sem,
           a_held, d_held, r_held, wd_high, wd_low, g_out, g_in, part, part_out, part_in, m_out, m_in,
           a_send, a_recv, d_send, d_recv, r_send, r_recv, g_send, g_recv, p_send, p_recv, m_send, m_recv):
    state = lax.axis_index("state")
    snap = lax.axis_index("snap")
    far, near = snap // near_count, snap % near_count
    rows, width = a_hbm.shape[2], a_hbm.shape[3]
    cells = far_count * near_count * rows
    modes = r_hbm.shape[1]
    slab = far_count // chunks

    def near_of(k):
        return lax.rem(near + k, near_count)

    def snap_of(far_at, near_at):
        return far_at * near_count + near_at

    barrier = pltpu.get_barrier_semaphore()

    def greet(k, carry):
        other = lax.rem(state + k // near_count, far_count)
        beside = lax.rem(near + k % near_count, near_count)
        pl.semaphore_signal(barrier, inc=1, device_id=(other, snap_of(far, beside)), device_id_type=MESH)
        return carry

    lax.fori_loop(1, far_count * near_count, greet, 0)

    def greet_far(k, carry):
        pl.semaphore_signal(barrier, inc=1, device_id=(state, snap_of(lax.rem(far + k, far_count), near)), device_id_type=MESH)
        return carry

    lax.fori_loop(1, far_count, greet_far, 0)
    loads = [
        pltpu.make_async_copy(src, dst, load_sem.at[i])
        for i, (src, dst) in enumerate((
            (l_hbm, l_ref), (root_hbm, root_ref), (a_hbm, a_ref), (w_hbm, w_ref),
            (d_hbm, d_held.at[near]), (r_hbm, r_held.at[near]),
        ))
    ]
    for load in loads:
        load.start()
    pl.semaphore_wait(barrier, far_count * near_count - 1 + far_count - 1)

    def a_copy(way, step, chunk, src, block):
        go = 1 if way == 0 else -1
        at = pl.ds(chunk * slab, slab)
        return pltpu.make_async_remote_copy(
            src_ref=src.at[at],
            dst_ref=a_held.at[block, at],
            send_sem=a_send.at[way, step, chunk],
            recv_sem=a_recv.at[way, step, chunk],
            device_id=(state, snap_of(jnp.clip(far + go, 0, far_count - 1), near)),
            device_id_type=MESH,
        )

    has_next = (far < far_count - 1, far > 0)

    for chunk in range(chunks):
        for way in range(2):
            @pl.when(has_next[way])
            def _():
                a_copy(way, 0, chunk, a_hbm, far).start()

    def d_copy(k):
        return pltpu.make_async_remote_copy(
            src_ref=d_hbm, dst_ref=d_held.at[near], send_sem=d_send.at[k], recv_sem=d_recv.at[k],
            device_id=(state, snap_of(far, near_of(k))), device_id_type=MESH)

    def r_copy(k):
        return pltpu.make_async_remote_copy(
            src_ref=r_hbm, dst_ref=r_held.at[near], send_sem=r_send.at[k], recv_sem=r_recv.at[k],
            device_id=(state, snap_of(far, near_of(k))), device_id_type=MESH)

    def p_copy(k):
        return pltpu.make_async_remote_copy(
            src_ref=part_out.at[k], dst_ref=part_in.at[k], send_sem=p_send.at[k], recv_sem=p_recv.at[k],
            device_id=(state, snap_of(far, near_of(k))), device_id_type=MESH)

    for k in range(1, near_count):
        d_copy(k).start()
        r_copy(k).start()

    for load in loads:
        load.wait()
    root = root_ref[...]
    left = split(l_ref[...] * root)

    def adjoint_terms(near_at):
        x = a_ref[:, near_at].reshape(far_count * rows, width)
        return product(split(x), left, 1).reshape(far_count, rows, modes)

    for k in range(1, near_count):
        part_out[k] = adjoint_terms(near_of(k))
        p_copy(k).start()
    part[...] = adjoint_terms(near)

    def pass_on(step):
        for chunk in range(chunks):
            for way in range(2):
                block = far - step if way == 0 else far + step
                held = jnp.clip(block, 0, far_count - 1)

                @pl.when((block >= 0) & (block < far_count))
                def _():
                    a_copy(way, step - 1, chunk, a_ref, held).wait_recv()

                    @pl.when(has_next[way])
                    def _():
                        a_copy(way, step, chunk, a_held.at[held], held).start()

    def g_copy(block, beside):
        return pltpu.make_async_remote_copy(
            src_ref=g_out.at[block, beside], dst_ref=g_in.at[state, near],
            send_sem=g_send.at[block, beside], recv_sem=g_recv.at[state, near],
            device_id=(block, snap_of(far, beside)), device_id_type=MESH)

    def gram_block(value, block):
        x = split(value.reshape(cells, width))
        whole = product(x, (wd_high[...], wd_low[...]), 0)
        for beside in range(near_count):
            piece = whole[:, beside * width:(beside + 1) * width]
            own = (block == state) & (beside == near)

            @pl.when(own)
            def _():
                g_in[state, near] = piece

            @pl.when(jnp.logical_not(own))
            def _():
                g_out[block, beside] = piece
                g_copy(block, beside).start()

    def gram_step(step):
        for way in range(2):
            block = far - step if way == 0 else far + step
            held = jnp.clip(block, 0, far_count - 1)

            @pl.when((block >= 0) & (block < far_count))
            def _():
                gram_block(a_held[held], held)

    pass_on(1)

    for k in range(1, near_count):
        d_copy(k).wait_recv()
    weight = jnp.broadcast_to(w_ref[...], (width, cells)).T
    for beside in range(near_count):
        high, low = split(d_held[beside].reshape(cells, width) * weight)
        wd_high[:, beside * width:(beside + 1) * width] = high
        wd_low[:, beside * width:(beside + 1) * width] = low
    gram_block(a_ref[...], far)
    gram_step(1)
    if far_count > 2:
        pass_on(2)

    for k in range(1, near_count):
        r_copy(k).wait_recv()
    total = None
    for beside in range(near_count):
        x = d_held[beside, :, near].reshape(far_count * rows, width)
        term = product(split(x), split(r_held[beside] * root), 1)
        total = term if total is None else total + term
    m_out[:, 0] = total.reshape(far_count, rows, modes)
    total = part[...]
    for k in range(1, near_count):
        p_copy(k).wait_recv()
        total = total + part_in[k]
    m_out[:, 1] = total

    def m_copy(k):
        other = lax.rem(far + k, far_count)
        return pltpu.make_async_remote_copy(
            src_ref=m_out.at[other], dst_ref=m_in.at[k], send_sem=m_send.at[k], recv_sem=m_recv.at[k],
            device_id=(state, snap_of(other, near)), device_id_type=MESH)

    def each_far(first, body):
        def step(k, carry):
            body(k)
            return carry

        lax.fori_loop(first, far_count, step, 0)

    each_far(1, lambda k: m_copy(k).start())

    if far_count > 2:
        gram_step(2)

    def later(step):
        pass_on(step)
        gram_step(step)

    each_far(3, later)

    m_in[0] = m_out[far]
    each_far(1, lambda k: m_copy(k).wait_recv())
    bal_ref[...] = jnp.sum(m_in[:, 0], axis=0)
    adj_ref[...] = jnp.sum(m_in[:, 1], axis=0)

    def g_wait(k):
        source, beside = k // near_count, k % near_count

        @pl.when((source != state) | (beside != near))
        def _():
            pltpu.make_async_remote_copy(
                src_ref=g_out.at[source, beside], dst_ref=g_in.at[source, beside],
                send_sem=g_send.at[source, beside], recv_sem=g_recv.at[source, beside],
                device_id=(source, snap_of(far, beside)), device_id_type=MESH).wait_recv()

    lax.fori_loop(0, far_count * near_count, lambda k, c: (g_wait(k), c)[1], 0)
    for beside in range(near_count):
        gram_ref[beside] = jnp.sum(g_in[:, beside], axis=0)

    for k in range(1, near_count):
        d_copy(k).wait_send()
        r_copy(k).wait_send()
        p_copy(k).wait_send()
    each_far(1, lambda k: m_copy(k).wait_send())

    def g_left(k):
        block, beside = k // near_count, k % near_count

        @pl.when((block != state) | (beside != near))
        def _():
            g_copy(block, beside).wait_send()

    lax.fori_loop(0, far_count * near_count, lambda k, c: (g_left(k), c)[1], 0)

    def a_left(step):
        for chunk in range(chunks):
            for way in range(2):
                block = far - step if way == 0 else far + step

                @pl.when((block >= 0) & (block < far_count) & has_next[way])
                def _():
                    a_copy(way, step, chunk, a_ref, far).wait_send()

    each_far(0, a_left)


def deliver(gram_ref, bal_ref, adj_ref, gram_out, bal_out, adj_out, sem):
    pairs = ((gram_ref, gram_out), (bal_ref, bal_out), (adj_ref, adj_out))
    copies = [pltpu.make_async_copy(src, dst, sem.at[i]) for i, (src, dst) in enumerate(pairs)]
    for copy in copies:
        copy.start()
    for copy in copies:
        copy.wait()


def local(direct, adjoint, cell_weight, right_vecs, left_vecs, inv_root):
    far_count = lax.axis_size("state")
    near_count = lax.axis_size("snap") // far_count
    cells, width = direct.shape
    modes = right_vecs.shape[1]
    rows = cells // (far_count * near_count)
    chunks = math.gcd(far_count, 4)
    block = (far_count, near_count, rows, width)
    vmem = pl.BlockSpec(memory_space=pltpu.VMEM)
    dma = pltpu.SemaphoreType.DMA
    hbm = pl.BlockSpec(memory_space=pltpu.HBM)
    results = pl.pallas_call(
        functools.partial(kernel, far_count, near_count, chunks),
        out_shape=(
            jax.ShapeDtypeStruct((near_count, width, width), F32),
            jax.ShapeDtypeStruct((rows, modes), F32),
            jax.ShapeDtypeStruct((rows, modes), F32),
        ),
        in_specs=[hbm] * 6,
        out_specs=(vmem,) * 3,
        scratch_shapes=[
            pltpu.VMEM(block, F32),
            pltpu.VMEM((width, modes), F32),
            pltpu.VMEM((1, cells), F32),
            pltpu.VMEM((1, modes), F32),
            dma((6,)),
            pltpu.VMEM((far_count,) + block, F32),
            pltpu.VMEM((near_count,) + block, F32),
            pltpu.VMEM((near_count, width, modes), F32),
            pltpu.VMEM((cells, near_count * width), BF16),
            pltpu.VMEM((cells, near_count * width), BF16),
            pltpu.VMEM((far_count, near_count, width, width), F32),
            pltpu.VMEM((far_count, near_count, width, width), F32),
            pltpu.VMEM((far_count, rows, modes), F32),
            pltpu.VMEM((near_count, far_count, rows, modes), F32),
            pltpu.VMEM((near_count, far_count, rows, modes), F32),
            pltpu.VMEM((far_count, 2, rows, modes), F32),
            pltpu.VMEM((far_count, 2, rows, modes), F32),
            dma((2, far_count, chunks)),
            dma((2, far_count, chunks)),
            dma((near_count,)),
            dma((near_count,)),
            dma((near_count,)),
            dma((near_count,)),
            dma((far_count, near_count)),
            dma((far_count, near_count)),
            dma((near_count,)),
            dma((near_count,)),
            dma((far_count,)),
            dma((far_count,)),
        ],
        compiler_params=pltpu.CompilerParams(
            collective_id=0, has_side_effects=True, vmem_limit_bytes=63 * 1024 * 1024
        ),
    )(
        adjoint.reshape(block),
        direct.reshape(block),
        cell_weight.reshape(1, cells),
        right_vecs,
        left_vecs,
        inv_root.reshape(1, modes),
    )
    gram, bal, adj = pl.pallas_call(
        deliver,
        out_shape=tuple(jax.ShapeDtypeStruct(r.shape, F32) for r in results),
        in_specs=[hbm] * 3,
        out_specs=(hbm,) * 3,
        scratch_shapes=[dma((3,))],
        compiler_params=pltpu.CompilerParams(vmem_limit_bytes=63 * 1024 * 1024),
    )(*results)
    return gram.reshape(near_count * width, width), bal, adj


def solution(mesh):
    in_specs = (
        P("state", "snap"),
        P("state", "snap"),
        P("state"),
        P("snap", None),
        P("snap", None),
        P(),
    )
    out_specs = (P("state", "snap"), P(("state", "snap"), None), P(("state", "snap"), None))
    return jax.shard_map(local, mesh=mesh, in_specs=in_specs, out_specs=out_specs, check_vma=False)
```

```python
import functools
import math

import jax
import jax.numpy as jnp
from jax import lax
from jax.experimental import pallas as pl
from jax.experimental.pallas import tpu as pltpu
from jax.sharding import PartitionSpec as P

MESH = pl.DeviceIdType.MESH
F32 = jnp.float32
BF16 = jnp.bfloat16


def split(x):
    high = x.astype(BF16)
    return high, (x - high.astype(F32)).astype(BF16)


def product(a, b, side):
    def one(x, y):
        return lax.dot_general(x, y, (((side,), (0,)), ((), ())), preferred_element_type=F32)

    return one(a[0], b[0]) + (one(a[0], b[1]) + one(a[1], b[0]))


def kernel(far_count, near_count, chunks, a_hbm, d_hbm, w_hbm, r_hbm, l_hbm, root_hbm,
           gram_ref, bal_ref, adj_ref, a_ref, l_ref, w_ref, root_ref, load_sem,
           a_held, d_held, r_held, wd_high, wd_low, g_out, g_in, part, part_out, part_in, m_out, m_in, sums,
           a_send, a_recv, d_send, d_recv, r_send, r_recv, g_send, g_recv, p_send, p_recv, m_send, m_recv):
    state = lax.axis_index("state")
    snap = lax.axis_index("snap")
    far, near = snap // near_count, snap % near_count
    rows, width = a_hbm.shape[2], a_hbm.shape[3]
    cells = far_count * near_count * rows
    modes = r_hbm.shape[1]
    slab = far_count // chunks

    def near_of(k):
        return lax.rem(near + k, near_count)

    def snap_of(far_at, near_at):
        return far_at * near_count + near_at

    barrier = pltpu.get_barrier_semaphore()

    def greet(k, carry):
        other = lax.rem(state + k // near_count, far_count)
        beside = lax.rem(near + k % near_count, near_count)
        pl.semaphore_signal(barrier, inc=1, device_id=(other, snap_of(far, beside)), device_id_type=MESH)
        return carry

    lax.fori_loop(1, far_count * near_count, greet, 0)

    def greet_far(k, carry):
        pl.semaphore_signal(barrier, inc=1, device_id=(state, snap_of(lax.rem(far + k, far_count), near)), device_id_type=MESH)
        return carry

    lax.fori_loop(1, far_count, greet_far, 0)
    loads = [
        pltpu.make_async_copy(src, dst, load_sem.at[i])
        for i, (src, dst) in enumerate((
            (l_hbm, l_ref), (root_hbm, root_ref), (a_hbm, a_ref), (w_hbm, w_ref),
            (d_hbm, d_held.at[near]), (r_hbm, r_held.at[near]),
        ))
    ]
    for load in loads:
        load.start()
    pl.semaphore_wait(barrier, far_count * near_count - 1 + far_count - 1)

    def a_copy(way, step, chunk, src, block):
        go = 1 if way == 0 else -1
        at = pl.ds(chunk * slab, slab)
        return pltpu.make_async_remote_copy(
            src_ref=src.at[at],
            dst_ref=a_held.at[block, at],
            send_sem=a_send.at[way, step, chunk],
            recv_sem=a_recv.at[way, step, chunk],
            device_id=(state, snap_of(jnp.clip(far + go, 0, far_count - 1), near)),
            device_id_type=MESH,
        )

    has_next = (far < far_count - 1, far > 0)

    for chunk in range(chunks):
        for way in range(2):
            @pl.when(has_next[way])
            def _():
                a_copy(way, 0, chunk, a_hbm, far).start()

    def d_copy(k):
        return pltpu.make_async_remote_copy(
            src_ref=d_hbm, dst_ref=d_held.at[near], send_sem=d_send.at[k], recv_sem=d_recv.at[k],
            device_id=(state, snap_of(far, near_of(k))), device_id_type=MESH)

    def r_copy(k):
        return pltpu.make_async_remote_copy(
            src_ref=r_hbm, dst_ref=r_held.at[near], send_sem=r_send.at[k], recv_sem=r_recv.at[k],
            device_id=(state, snap_of(far, near_of(k))), device_id_type=MESH)

    def p_copy(k):
        return pltpu.make_async_remote_copy(
            src_ref=part_out.at[k], dst_ref=part_in.at[k], send_sem=p_send.at[k], recv_sem=p_recv.at[k],
            device_id=(state, snap_of(far, near_of(k))), device_id_type=MESH)

    for k in range(1, near_count):
        d_copy(k).start()
        r_copy(k).start()

    for load in loads:
        load.wait()
    root = root_ref[...]
    left = split(l_ref[...] * root)

    def adjoint_terms(near_at):
        x = a_ref[:, near_at].reshape(far_count * rows, width)
        return product(split(x), left, 1).reshape(far_count, rows, modes)

    for k in range(1, near_count):
        part_out[k] = adjoint_terms(near_of(k))
        p_copy(k).start()
    part[...] = adjoint_terms(near)

    def pass_on(step):
        for chunk in range(chunks):
            for way in range(2):
                block = far - step if way == 0 else far + step
                held = jnp.clip(block, 0, far_count - 1)

                @pl.when((block >= 0) & (block < far_count))
                def _():
                    a_copy(way, step - 1, chunk, a_ref, held).wait_recv()

                    @pl.when(has_next[way])
                    def _():
                        a_copy(way, step, chunk, a_held.at[held], held).start()

    def g_copy(block, beside):
        return pltpu.make_async_remote_copy(
            src_ref=g_out.at[block, beside], dst_ref=g_in.at[state, near],
            send_sem=g_send.at[block, beside], recv_sem=g_recv.at[state, near],
            device_id=(block, snap_of(far, beside)), device_id_type=MESH)

    def gram_block(value, block):
        x = split(value.reshape(cells, width))
        hand_out(product(x, (wd_high[...], wd_low[...]), 0), block)

    def hand_out(whole, block):
        for beside in range(near_count):
            piece = whole[:, beside * width:(beside + 1) * width]
            own = (block == state) & (beside == near)

            @pl.when(own)
            def _():
                g_in[state, near] = piece

            @pl.when(jnp.logical_not(own))
            def _():
                g_out[block, beside] = piece
                g_copy(block, beside).start()

    def pass_and_add(step):
        for chunk in range(chunks):
            for way in range(2):
                block = far - step if way == 0 else far + step
                held = jnp.clip(block, 0, far_count - 1)

                @pl.when((block >= 0) & (block < far_count))
                def _():
                    a_copy(way, step - 1, chunk, a_ref, held).wait_recv()

                    @pl.when(has_next[way])
                    def _():
                        a_copy(way, step, chunk, a_held.at[held], held).start()

                    size = cells // chunks
                    x = split(a_held[held, pl.ds(chunk * slab, slab)].reshape(size, width))
                    at = pl.ds(chunk * size, size)
                    terms = product(x, (wd_high[at], wd_low[at]), 0)
                    if chunk > 0:
                        terms = terms + sums[way]
                    if chunk < chunks - 1:
                        sums[way] = terms
                    else:
                        hand_out(terms, held)

    def gram_step(step):
        for way in range(2):
            block = far - step if way == 0 else far + step
            held = jnp.clip(block, 0, far_count - 1)

            @pl.when((block >= 0) & (block < far_count))
            def _():
                gram_block(a_held[held], held)

    pass_on(1)

    for k in range(1, near_count):
        d_copy(k).wait_recv()
    weight = jnp.broadcast_to(w_ref[...], (width, cells)).T
    for beside in range(near_count):
        high, low = split(d_held[beside].reshape(cells, width) * weight)
        wd_high[:, beside * width:(beside + 1) * width] = high
        wd_low[:, beside * width:(beside + 1) * width] = low
    gram_block(a_ref[...], far)
    gram_step(1)
    if far_count > 2:
        pass_and_add(2)

    for k in range(1, near_count):
        r_copy(k).wait_recv()
    total = None
    for beside in range(near_count):
        x = d_held[beside, :, near].reshape(far_count * rows, width)
        term = product(split(x), split(r_held[beside] * root), 1)
        total = term if total is None else total + term
    m_out[:, 0] = total.reshape(far_count, rows, modes)
    total = part[...]
    for k in range(1, near_count):
        p_copy(k).wait_recv()
        total = total + part_in[k]
    m_out[:, 1] = total

    def m_copy(way, at, src):
        go = 1 if way == 0 else -1
        return pltpu.make_async_remote_copy(
            src_ref=src, dst_ref=m_in.at[way, at], send_sem=m_send.at[way, at], recv_sem=m_recv.at[way, at],
            device_id=(state, snap_of(jnp.clip(far + go, 0, far_count - 1), near)), device_id_type=MESH)

    has_before = (has_next[1], has_next[0])

    def each_far(first, body):
        def step(k, carry):
            body(k)
            return carry

        lax.fori_loop(first, far_count, step, 0)

    def stage(k):
        for way in range(2):
            @pl.when(far == (k if way == 0 else far_count - 1 - k))
            def _():
                def one(j):
                    at = far_count - j if way == 0 else j - 1
                    beyond = at > far if way == 0 else at < far

                    @pl.when(beyond & has_before[way])
                    def _():
                        m_copy(way, at, m_out.at[at]).wait_recv()
                        m_in[way, at] = m_in[way, at] + m_out[at]
                        m_copy(way, at, m_in.at[way, at]).start()

                    @pl.when(beyond & jnp.logical_not(has_before[way]))
                    def _():
                        m_copy(way, at, m_out.at[at]).start()

                each_far_from_one(one)

    def each_far_from_one(body):
        lax.fori_loop(1, far_count + 1, lambda j, c: (body(j), c)[1], 0)

    stage(0)

    def later(step):
        pass_and_add(step)
        stage(step - 2)

    each_far(3, later)
    if far_count > 2:
        stage(far_count - 2)

    m_out_own = m_out[far]
    for way in range(2):
        @pl.when(has_before[way])
        def _():
            m_copy(way, far, m_out.at[far]).wait_recv()

        @pl.when(jnp.logical_not(has_before[way]))
        def _():
            m_in[way, far] = jnp.zeros_like(m_in[way, far])

        m_out_own = m_out_own + m_in[way, far]
    bal_ref[...] = m_out_own[0]
    adj_ref[...] = m_out_own[1]

    def g_wait(k):
        source, beside = k // near_count, k % near_count

        @pl.when((source != state) | (beside != near))
        def _():
            pltpu.make_async_remote_copy(
                src_ref=g_out.at[source, beside], dst_ref=g_in.at[source, beside],
                send_sem=g_send.at[source, beside], recv_sem=g_recv.at[source, beside],
                device_id=(source, snap_of(far, beside)), device_id_type=MESH).wait_recv()

    lax.fori_loop(0, far_count * near_count, lambda k, c: (g_wait(k), c)[1], 0)
    for beside in range(near_count):
        gram_ref[beside] = jnp.sum(g_in[:, beside], axis=0)

    for k in range(1, near_count):
        d_copy(k).wait_send()
        r_copy(k).wait_send()
        p_copy(k).wait_send()

    def m_left(at):
        for way in range(2):
            @pl.when(at > far if way == 0 else at < far)
            def _():
                m_copy(way, at, m_out.at[at]).wait_send()

    each_far(0, m_left)

    def g_left(k):
        block, beside = k // near_count, k % near_count

        @pl.when((block != state) | (beside != near))
        def _():
            g_copy(block, beside).wait_send()

    lax.fori_loop(0, far_count * near_count, lambda k, c: (g_left(k), c)[1], 0)

    def a_left(step):
        for chunk in range(chunks):
            for way in range(2):
                block = far - step if way == 0 else far + step

                @pl.when((block >= 0) & (block < far_count) & has_next[way])
                def _():
                    a_copy(way, step, chunk, a_ref, far).wait_send()

    each_far(0, a_left)


def local(direct, adjoint, cell_weight, right_vecs, left_vecs, inv_root):
    far_count = lax.axis_size("state")
    near_count = lax.axis_size("snap") // far_count
    cells, width = direct.shape
    modes = right_vecs.shape[1]
    rows = cells // (far_count * near_count)
    chunks = math.gcd(far_count, 4)
    block = (far_count, near_count, rows, width)
    vmem = pl.BlockSpec(memory_space=pltpu.VMEM)
    dma = pltpu.SemaphoreType.DMA
    hbm = pl.BlockSpec(memory_space=pltpu.HBM)
    gram, bal, adj = pl.pallas_call(
        functools.partial(kernel, far_count, near_count, chunks),
        out_shape=(
            jax.ShapeDtypeStruct((near_count, width, width), F32),
            jax.ShapeDtypeStruct((rows, modes), F32),
            jax.ShapeDtypeStruct((rows, modes), F32),
        ),
        in_specs=[hbm] * 6,
        out_specs=(vmem,) * 3,
        scratch_shapes=[
            pltpu.VMEM(block, F32),
            pltpu.VMEM((width, modes), F32),
            pltpu.VMEM((1, cells), F32),
            pltpu.VMEM((1, modes), F32),
            dma((6,)),
            pltpu.VMEM((far_count,) + block, F32),
            pltpu.VMEM((near_count,) + block, F32),
            pltpu.VMEM((near_count, width, modes), F32),
            pltpu.VMEM((cells, near_count * width), BF16),
            pltpu.VMEM((cells, near_count * width), BF16),
            pltpu.VMEM((far_count, near_count, width, width), F32),
            pltpu.VMEM((far_count, near_count, width, width), F32),
            pltpu.VMEM((far_count, rows, modes), F32),
            pltpu.VMEM((near_count, far_count, rows, modes), F32),
            pltpu.VMEM((near_count, far_count, rows, modes), F32),
            pltpu.VMEM((far_count, 2, rows, modes), F32),
            pltpu.VMEM((2, far_count, 2, rows, modes), F32),
            pltpu.VMEM((2, width, near_count * width), F32),
            dma((2, far_count, chunks)),
            dma((2, far_count, chunks)),
            dma((near_count,)),
            dma((near_count,)),
            dma((near_count,)),
            dma((near_count,)),
            dma((far_count, near_count)),
            dma((far_count, near_count)),
            dma((near_count,)),
            dma((near_count,)),
            dma((2, far_count)),
            dma((2, far_count)),
        ],
        compiler_params=pltpu.CompilerParams(
            collective_id=0, has_side_effects=True, vmem_limit_bytes=63 * 1024 * 1024
        ),
    )(
        adjoint.reshape(block),
        direct.reshape(block),
        cell_weight.reshape(1, cells),
        right_vecs,
        left_vecs,
        inv_root.reshape(1, modes),
    )
    return gram.reshape(near_count * width, width), bal, adj


def solution(mesh):
    in_specs = (
        P("state", "snap"),
        P("state", "snap"),
        P("state"),
        P("snap", None),
        P("snap", None),
        P(),
    )
    out_specs = (P("state", "snap"), P(("state", "snap"), None), P(("state", "snap"), None))
    return jax.shard_map(local, mesh=mesh, in_specs=in_specs, out_specs=out_specs, check_vma=False)
```

```python
import functools
import math

import jax
import jax.numpy as jnp
from jax import lax
from jax.experimental import pallas as pl
from jax.experimental.pallas import tpu as pltpu
from jax.sharding import PartitionSpec as P

MESH = pl.DeviceIdType.MESH
F32 = jnp.float32
BF16 = jnp.bfloat16


def split(x):
    high = x.astype(BF16)
    return high, (x - high.astype(F32)).astype(BF16)


def product(a, b, side):
    def one(x, y):
        return lax.dot_general(x, y, (((side,), (0,)), ((), ())), preferred_element_type=F32)

    return one(a[0], b[0]) + (one(a[0], b[1]) + one(a[1], b[0]))


def kernel(far_count, near_count, chunks, a_hbm, d_hbm, w_hbm, r_hbm, l_hbm, root_hbm,
           gram_ref, bal_ref, adj_ref, a_ref, l_ref, w_ref, root_ref, load_sem,
           a_held, d_held, r_held, wd_high, wd_low, g_out, g_in, part, part_out, part_in, m_out, m_in,
           a_send, a_recv, d_send, d_recv, r_send, r_recv, g_send, g_recv, p_send, p_recv, m_send, m_recv):
    state = lax.axis_index("state")
    snap = lax.axis_index("snap")
    far, near = snap // near_count, snap % near_count
    rows, width = a_hbm.shape[2], a_hbm.shape[3]
    cells = far_count * near_count * rows
    modes = r_hbm.shape[1]
    slab = far_count // chunks

    def near_of(k):
        return lax.rem(near + k, near_count)

    def snap_of(far_at, near_at):
        return far_at * near_count + near_at

    barrier = pltpu.get_barrier_semaphore()

    def greet(k, carry):
        other = lax.rem(state + k // near_count, far_count)
        beside = lax.rem(near + k % near_count, near_count)
        pl.semaphore_signal(barrier, inc=1, device_id=(other, snap_of(far, beside)), device_id_type=MESH)
        return carry

    lax.fori_loop(1, far_count * near_count, greet, 0)

    def greet_far(k, carry):
        pl.semaphore_signal(barrier, inc=1, device_id=(state, snap_of(lax.rem(far + k, far_count), near)), device_id_type=MESH)
        return carry

    lax.fori_loop(1, far_count, greet_far, 0)
    loads = [
        pltpu.make_async_copy(src, dst, load_sem.at[i])
        for i, (src, dst) in enumerate((
            (l_hbm, l_ref), (root_hbm, root_ref), (a_hbm, a_ref), (w_hbm, w_ref),
            (d_hbm, d_held.at[near]), (r_hbm, r_held.at[near]),
        ))
    ]
    for load in loads:
        load.start()
    pl.semaphore_wait(barrier, far_count * near_count - 1 + far_count - 1)

    def a_copy(way, step, chunk, src, block):
        go = 1 if way == 0 else -1
        at = pl.ds(chunk * slab, slab)
        return pltpu.make_async_remote_copy(
            src_ref=src.at[at],
            dst_ref=a_held.at[block, at],
            send_sem=a_send.at[way, step, chunk],
            recv_sem=a_recv.at[way, step, chunk],
            device_id=(state, snap_of(jnp.clip(far + go, 0, far_count - 1), near)),
            device_id_type=MESH,
        )

    has_next = (far < far_count - 1, far > 0)

    for chunk in range(chunks):
        for way in range(2):
            @pl.when(has_next[way])
            def _():
                a_copy(way, 0, chunk, a_hbm, far).start()

    def d_copy(k):
        return pltpu.make_async_remote_copy(
            src_ref=d_hbm, dst_ref=d_held.at[near], send_sem=d_send.at[k], recv_sem=d_recv.at[k],
            device_id=(state, snap_of(far, near_of(k))), device_id_type=MESH)

    def r_copy(k):
        return pltpu.make_async_remote_copy(
            src_ref=r_hbm, dst_ref=r_held.at[near], send_sem=r_send.at[k], recv_sem=r_recv.at[k],
            device_id=(state, snap_of(far, near_of(k))), device_id_type=MESH)

    def p_copy(k):
        return pltpu.make_async_remote_copy(
            src_ref=part_out.at[k], dst_ref=part_in.at[k], send_sem=p_send.at[k], recv_sem=p_recv.at[k],
            device_id=(state, snap_of(far, near_of(k))), device_id_type=MESH)

    for k in range(1, near_count):
        d_copy(k).start()
        r_copy(k).start()

    for load in loads:
        load.wait()
    root = root_ref[...]
    left = split(l_ref[...] * root)

    def adjoint_terms(near_at):
        x = a_ref[:, near_at].reshape(far_count * rows, width)
        return product(split(x), left, 1).reshape(far_count, rows, modes)

    for k in range(1, near_count):
        part_out[k] = adjoint_terms(near_of(k))
        p_copy(k).start()
    part[...] = adjoint_terms(near)

    def pass_on(step):
        for chunk in range(chunks):
            for way in range(2):
                block = far - step if way == 0 else far + step
                held = jnp.clip(block, 0, far_count - 1)

                @pl.when((block >= 0) & (block < far_count))
                def _():
                    a_copy(way, step - 1, chunk, a_ref, held).wait_recv()

                    @pl.when(has_next[way])
                    def _():
                        a_copy(way, step, chunk, a_held.at[held], held).start()

    def g_copy(block, beside):
        return pltpu.make_async_remote_copy(
            src_ref=g_out.at[block, beside], dst_ref=g_in.at[state, near],
            send_sem=g_send.at[block, beside], recv_sem=g_recv.at[state, near],
            device_id=(block, snap_of(far, beside)), device_id_type=MESH)

    def gram_block(value, block):
        x = split(value.reshape(cells, width))
        whole = product(x, (wd_high[...], wd_low[...]), 0)
        for beside in range(near_count):
            piece = whole[:, beside * width:(beside + 1) * width]
            own = (block == state) & (beside == near)

            @pl.when(own)
            def _():
                g_in[state, near] = piece

            @pl.when(jnp.logical_not(own))
            def _():
                g_out[block, beside] = piece
                g_copy(block, beside).start()

    def gram_step(step):
        for way in range(2):
            block = far - step if way == 0 else far + step
            held = jnp.clip(block, 0, far_count - 1)

            @pl.when((block >= 0) & (block < far_count))
            def _():
                gram_block(a_held[held], held)

    pass_on(1)

    for k in range(1, near_count):
        d_copy(k).wait_recv()
    weight = jnp.broadcast_to(w_ref[...], (width, cells)).T
    for beside in range(near_count):
        high, low = split(d_held[beside].reshape(cells, width) * weight)
        wd_high[:, beside * width:(beside + 1) * width] = high
        wd_low[:, beside * width:(beside + 1) * width] = low
    gram_block(a_ref[...], far)
    gram_step(1)
    if far_count > 2:
        pass_on(2)

    for k in range(1, near_count):
        r_copy(k).wait_recv()
    total = None
    for beside in range(near_count):
        x = d_held[beside, :, near].reshape(far_count * rows, width)
        term = product(split(x), split(r_held[beside] * root), 1)
        total = term if total is None else total + term
    m_out[:, 0] = total.reshape(far_count, rows, modes)
    total = part[...]
    for k in range(1, near_count):
        p_copy(k).wait_recv()
        total = total + part_in[k]
    m_out[:, 1] = total

    def m_copy(k):
        other = lax.rem(far + k, far_count)
        return pltpu.make_async_remote_copy(
            src_ref=m_out.at[other], dst_ref=m_in.at[k], send_sem=m_send.at[k], recv_sem=m_recv.at[k],
            device_id=(state, snap_of(other, near)), device_id_type=MESH)

    def each_far(first, body):
        def step(k, carry):
            body(k)
            return carry

        lax.fori_loop(first, far_count, step, 0)

    each_far(1, lambda k: m_copy(k).start())

    if far_count > 2:
        gram_step(2)

    def later(step):
        pass_on(step)
        gram_step(step)

    each_far(3, later)

    m_in[0] = m_out[far]
    each_far(1, lambda k: m_copy(k).wait_recv())
    bal_ref[...] = jnp.sum(m_in[:, 0], axis=0)
    adj_ref[...] = jnp.sum(m_in[:, 1], axis=0)

    def g_wait(k):
        source, beside = k // near_count, k % near_count

        @pl.when((source != state) | (beside != near))
        def _():
            pltpu.make_async_remote_copy(
                src_ref=g_out.at[source, beside], dst_ref=g_in.at[source, beside],
                send_sem=g_send.at[source, beside], recv_sem=g_recv.at[source, beside],
                device_id=(source, snap_of(far, beside)), device_id_type=MESH).wait_recv()

    lax.fori_loop(0, far_count * near_count, lambda k, c: (g_wait(k), c)[1], 0)
    for beside in range(near_count):
        gram_ref[beside] = jnp.sum(g_in[:, beside], axis=0)

    for k in range(1, near_count):
        d_copy(k).wait_send()
        r_copy(k).wait_send()
        p_copy(k).wait_send()
    each_far(1, lambda k: m_copy(k).wait_send())

    def g_left(k):
        block, beside = k // near_count, k % near_count

        @pl.when((block != state) | (beside != near))
        def _():
            g_copy(block, beside).wait_send()

    lax.fori_loop(0, far_count * near_count, lambda k, c: (g_left(k), c)[1], 0)

    def a_left(step):
        for chunk in range(chunks):
            for way in range(2):
                block = far - step if way == 0 else far + step

                @pl.when((block >= 0) & (block < far_count) & has_next[way])
                def _():
                    a_copy(way, step, chunk, a_ref, far).wait_send()

    each_far(0, a_left)


def local(direct, adjoint, cell_weight, right_vecs, left_vecs, inv_root):
    far_count = lax.axis_size("state")
    near_count = lax.axis_size("snap") // far_count
    cells, width = direct.shape
    modes = right_vecs.shape[1]
    rows = cells // (far_count * near_count)
    chunks = math.gcd(far_count, 4)
    block = (far_count, near_count, rows, width)
    vmem = pl.BlockSpec(memory_space=pltpu.VMEM)
    dma = pltpu.SemaphoreType.DMA
    hbm = pl.BlockSpec(memory_space=pltpu.HBM)
    gram, bal, adj = pl.pallas_call(
        functools.partial(kernel, far_count, near_count, chunks),
        out_shape=(
            jax.ShapeDtypeStruct((near_count, width, width), F32),
            jax.ShapeDtypeStruct((rows, modes), F32),
            jax.ShapeDtypeStruct((rows, modes), F32),
        ),
        in_specs=[hbm] * 6,
        out_specs=(vmem,) * 3,
        scratch_shapes=[
            pltpu.VMEM(block, F32),
            pltpu.VMEM((width, modes), F32),
            pltpu.VMEM((1, cells), F32),
            pltpu.VMEM((1, modes), F32),
            dma((6,)),
            pltpu.VMEM((far_count,) + block, F32),
            pltpu.VMEM((near_count,) + block, F32),
            pltpu.VMEM((near_count, width, modes), F32),
            pltpu.VMEM((cells, near_count * width), BF16),
            pltpu.VMEM((cells, near_count * width), BF16),
            pltpu.VMEM((far_count, near_count, width, width), F32),
            pltpu.VMEM((far_count, near_count, width, width), F32),
            pltpu.VMEM((far_count, rows, modes), F32),
            pltpu.VMEM((near_count, far_count, rows, modes), F32),
            pltpu.VMEM((near_count, far_count, rows, modes), F32),
            pltpu.VMEM((far_count, 2, rows, modes), F32),
            pltpu.VMEM((far_count, 2, rows, modes), F32),
            dma((2, far_count, chunks)),
            dma((2, far_count, chunks)),
            dma((near_count,)),
            dma((near_count,)),
            dma((near_count,)),
            dma((near_count,)),
            dma((far_count, near_count)),
            dma((far_count, near_count)),
            dma((near_count,)),
            dma((near_count,)),
            dma((far_count,)),
            dma((far_count,)),
        ],
        compiler_params=pltpu.CompilerParams(
            collective_id=0, has_side_effects=True, vmem_limit_bytes=63 * 1024 * 1024
        ),
    )(
        adjoint.reshape(block),
        direct.reshape(block),
        cell_weight.reshape(1, cells),
        right_vecs,
        left_vecs,
        inv_root.reshape(1, modes),
    )
    return gram.reshape(near_count * width, width), bal, adj


def solution(mesh):
    in_specs = (
        P("state", "snap"),
        P("state", "snap"),
        P("state"),
        P("snap", None),
        P("snap", None),
        P(),
    )
    out_specs = (P("state", "snap"), P(("state", "snap"), None), P(("state", "snap"), None))
    return jax.shard_map(local, mesh=mesh, in_specs=in_specs, out_specs=out_specs, check_vma=False)
```

```python
import functools
import math

import jax
import jax.numpy as jnp
from jax import lax
from jax.experimental import pallas as pl
from jax.experimental.pallas import tpu as pltpu
from jax.sharding import PartitionSpec as P

MESH = pl.DeviceIdType.MESH
F32 = jnp.float32
BF16 = jnp.bfloat16


def split(x):
    high = x.astype(BF16)
    return high, (x - high.astype(F32)).astype(BF16)


def product(a, b, side):
    def one(x, y):
        return lax.dot_general(x, y, (((side,), (0,)), ((), ())), preferred_element_type=F32)

    return one(a[0], b[0]) + (one(a[0], b[1]) + one(a[1], b[0]))


def kernel(far_count, near_count, chunks, a_hbm, d_hbm, w_hbm, r_hbm, l_hbm, root_hbm,
           gram_ref, bal_ref, adj_ref, a_ref, l_ref, w_ref, root_ref, load_sem,
           a_held, d_held, r_held, wd_high, wd_low, g_out, g_in, part, part_out, part_in, m_out, m_in,
           a_send, a_recv, d_send, d_recv, r_send, r_recv, g_send, g_recv, p_send, p_recv, m_send, m_recv):
    state = lax.axis_index("state")
    snap = lax.axis_index("snap")
    far, near = snap // near_count, snap % near_count
    rows, width = a_hbm.shape[2], a_hbm.shape[3]
    cells = far_count * near_count * rows
    modes = r_hbm.shape[1]
    slab = far_count // chunks

    def near_of(k):
        return lax.rem(near + k, near_count)

    def snap_of(far_at, near_at):
        return far_at * near_count + near_at

    barrier = pltpu.get_barrier_semaphore()

    def greet(k, carry):
        other = lax.rem(state + k // near_count, far_count)
        beside = lax.rem(near + k % near_count, near_count)
        pl.semaphore_signal(barrier, inc=1, device_id=(other, snap_of(far, beside)), device_id_type=MESH)
        return carry

    lax.fori_loop(1, far_count * near_count, greet, 0)

    def greet_far(k, carry):
        pl.semaphore_signal(barrier, inc=1, device_id=(state, snap_of(lax.rem(far + k, far_count), near)), device_id_type=MESH)
        return carry

    lax.fori_loop(1, far_count, greet_far, 0)
    loads = [
        pltpu.make_async_copy(src, dst, load_sem.at[i])
        for i, (src, dst) in enumerate((
            (l_hbm, l_ref), (root_hbm, root_ref), (a_hbm, a_ref), (w_hbm, w_ref),
            (d_hbm, d_held.at[near]), (r_hbm, r_held.at[near]),
        ))
    ]
    for load in loads:
        load.start()
    pl.semaphore_wait(barrier, far_count * near_count - 1 + far_count - 1)

    def a_copy(way, step, chunk, src, block):
        go = 1 if way == 0 else -1
        at = pl.ds(chunk * slab, slab)
        return pltpu.make_async_remote_copy(
            src_ref=src.at[at],
            dst_ref=a_held.at[block, at],
            send_sem=a_send.at[way, step, chunk],
            recv_sem=a_recv.at[way, step, chunk],
            device_id=(state, snap_of(jnp.clip(far + go, 0, far_count - 1), near)),
            device_id_type=MESH,
        )

    has_next = (far < far_count - 1, far > 0)

    for chunk in range(chunks):
        for way in range(2):
            @pl.when(has_next[way])
            def _():
                a_copy(way, 0, chunk, a_hbm, far).start()

    def d_copy(k):
        return pltpu.make_async_remote_copy(
            src_ref=d_hbm, dst_ref=d_held.at[near], send_sem=d_send.at[k], recv_sem=d_recv.at[k],
            device_id=(state, snap_of(far, near_of(k))), device_id_type=MESH)

    def r_copy(k):
        return pltpu.make_async_remote_copy(
            src_ref=r_hbm, dst_ref=r_held.at[near], send_sem=r_send.at[k], recv_sem=r_recv.at[k],
            device_id=(state, snap_of(far, near_of(k))), device_id_type=MESH)

    def p_copy(k):
        return pltpu.make_async_remote_copy(
            src_ref=part_out.at[k], dst_ref=part_in.at[k], send_sem=p_send.at[k], recv_sem=p_recv.at[k],
            device_id=(state, snap_of(far, near_of(k))), device_id_type=MESH)

    for k in range(1, near_count):
        d_copy(k).start()
        r_copy(k).start()

    for load in loads:
        load.wait()
    root = root_ref[...]
    left = split(l_ref[...] * root)

    def adjoint_terms(near_at):
        x = a_ref[:, near_at].reshape(far_count * rows, width)
        return product(split(x), left, 1).reshape(far_count, rows, modes)

    for k in range(1, near_count):
        part_out[k] = adjoint_terms(near_of(k))
        p_copy(k).start()
    part[...] = adjoint_terms(near)

    def pass_on(step):
        for chunk in range(chunks):
            for way in range(2):
                block = far - step if way == 0 else far + step
                held = jnp.clip(block, 0, far_count - 1)

                @pl.when((block >= 0) & (block < far_count))
                def _():
                    a_copy(way, step - 1, chunk, a_ref, held).wait_recv()

                    @pl.when(has_next[way])
                    def _():
                        a_copy(way, step, chunk, a_held.at[held], held).start()

    def g_copy(block, beside):
        return pltpu.make_async_remote_copy(
            src_ref=g_out.at[block, beside], dst_ref=g_in.at[state, near],
            send_sem=g_send.at[block, beside], recv_sem=g_recv.at[state, near],
            device_id=(block, snap_of(far, beside)), device_id_type=MESH)

    def gram_block(value, block):
        x = split(value.reshape(cells, width))
        whole = product(x, (wd_high[...], wd_low[...]), 0)
        for beside in range(near_count):
            piece = whole[:, beside * width:(beside + 1) * width]
            own = (block == state) & (beside == near)

            @pl.when(own)
            def _():
                g_in[state, near] = piece

            @pl.when(jnp.logical_not(own))
            def _():
                g_out[block, beside] = piece
                g_copy(block, beside).start()

    def gram_step(step):
        for way in range(2):
            block = far - step if way == 0 else far + step
            held = jnp.clip(block, 0, far_count - 1)

            @pl.when((block >= 0) & (block < far_count))
            def _():
                gram_block(a_held[held], held)

    pass_on(1)

    for k in range(1, near_count):
        d_copy(k).wait_recv()
    weight = jnp.broadcast_to(w_ref[...], (width, cells)).T
    for beside in range(near_count):
        high, low = split(d_held[beside].reshape(cells, width) * weight)
        wd_high[:, beside * width:(beside + 1) * width] = high
        wd_low[:, beside * width:(beside + 1) * width] = low
    gram_block(a_ref[...], far)
    gram_step(1)
    if far_count > 2:
        pass_on(2)

    for k in range(1, near_count):
        r_copy(k).wait_recv()
    total = None
    for beside in range(near_count):
        x = d_held[beside, :, near].reshape(far_count * rows, width)
        term = product(split(x), split(r_held[beside] * root), 1)
        total = term if total is None else total + term
    m_out[:, 0] = total.reshape(far_count, rows, modes)
    total = part[...]
    for k in range(1, near_count):
        p_copy(k).wait_recv()
        total = total + part_in[k]
    m_out[:, 1] = total

    def m_copy(k):
        other = lax.rem(far + k, far_count)
        return pltpu.make_async_remote_copy(
            src_ref=m_out.at[other], dst_ref=m_in.at[k], send_sem=m_send.at[k], recv_sem=m_recv.at[k],
            device_id=(state, snap_of(other, near)), device_id_type=MESH)

    def each_far(first, body):
        def step(k, carry):
            body(k)
            return carry

        lax.fori_loop(first, far_count, step, 0)

    if far_count > 2:
        gram_step(2)

    def later(step):
        pass_on(step)
        gram_step(step)

    lax.fori_loop(3, far_count - 1, lambda k, c: (later(k), c)[1], 0)
    if far_count > 3:
        pass_on(far_count - 1)

    def a_left(step):
        for chunk in range(chunks):
            for way in range(2):
                block = far - step if way == 0 else far + step

                @pl.when((block >= 0) & (block < far_count) & has_next[way])
                def _():
                    a_copy(way, step, chunk, a_ref, far).wait_send()

    each_far(0, a_left)
    each_far(1, lambda k: m_copy(k).start())
    if far_count > 3:
        gram_step(far_count - 1)

    m_in[0] = m_out[far]
    each_far(1, lambda k: m_copy(k).wait_recv())
    bal_ref[...] = jnp.sum(m_in[:, 0], axis=0)
    adj_ref[...] = jnp.sum(m_in[:, 1], axis=0)

    def g_wait(k):
        source, beside = k // near_count, k % near_count

        @pl.when((source != state) | (beside != near))
        def _():
            pltpu.make_async_remote_copy(
                src_ref=g_out.at[source, beside], dst_ref=g_in.at[source, beside],
                send_sem=g_send.at[source, beside], recv_sem=g_recv.at[source, beside],
                device_id=(source, snap_of(far, beside)), device_id_type=MESH).wait_recv()

    lax.fori_loop(0, far_count * near_count, lambda k, c: (g_wait(k), c)[1], 0)
    for beside in range(near_count):
        gram_ref[beside] = jnp.sum(g_in[:, beside], axis=0)

    for k in range(1, near_count):
        d_copy(k).wait_send()
        r_copy(k).wait_send()
        p_copy(k).wait_send()
    each_far(1, lambda k: m_copy(k).wait_send())

    def g_left(k):
        block, beside = k // near_count, k % near_count

        @pl.when((block != state) | (beside != near))
        def _():
            g_copy(block, beside).wait_send()

    lax.fori_loop(0, far_count * near_count, lambda k, c: (g_left(k), c)[1], 0)


def local(direct, adjoint, cell_weight, right_vecs, left_vecs, inv_root):
    far_count = lax.axis_size("state")
    near_count = lax.axis_size("snap") // far_count
    cells, width = direct.shape
    modes = right_vecs.shape[1]
    rows = cells // (far_count * near_count)
    chunks = math.gcd(far_count, 4)
    block = (far_count, near_count, rows, width)
    vmem = pl.BlockSpec(memory_space=pltpu.VMEM)
    dma = pltpu.SemaphoreType.DMA
    hbm = pl.BlockSpec(memory_space=pltpu.HBM)
    gram, bal, adj = pl.pallas_call(
        functools.partial(kernel, far_count, near_count, chunks),
        out_shape=(
            jax.ShapeDtypeStruct((near_count, width, width), F32),
            jax.ShapeDtypeStruct((rows, modes), F32),
            jax.ShapeDtypeStruct((rows, modes), F32),
        ),
        in_specs=[hbm] * 6,
        out_specs=(vmem,) * 3,
        scratch_shapes=[
            pltpu.VMEM(block, F32),
            pltpu.VMEM((width, modes), F32),
            pltpu.VMEM((1, cells), F32),
            pltpu.VMEM((1, modes), F32),
            dma((6,)),
            pltpu.VMEM((far_count,) + block, F32),
            pltpu.VMEM((near_count,) + block, F32),
            pltpu.VMEM((near_count, width, modes), F32),
            pltpu.VMEM((cells, near_count * width), BF16),
            pltpu.VMEM((cells, near_count * width), BF16),
            pltpu.VMEM((far_count, near_count, width, width), F32),
            pltpu.VMEM((far_count, near_count, width, width), F32),
            pltpu.VMEM((far_count, rows, modes), F32),
            pltpu.VMEM((near_count, far_count, rows, modes), F32),
            pltpu.VMEM((near_count, far_count, rows, modes), F32),
            pltpu.VMEM((far_count, 2, rows, modes), F32),
            pltpu.VMEM((far_count, 2, rows, modes), F32),
            dma((2, far_count, chunks)),
            dma((2, far_count, chunks)),
            dma((near_count,)),
            dma((near_count,)),
            dma((near_count,)),
            dma((near_count,)),
            dma((far_count, near_count)),
            dma((far_count, near_count)),
            dma((near_count,)),
            dma((near_count,)),
            dma((far_count,)),
            dma((far_count,)),
        ],
        compiler_params=pltpu.CompilerParams(
            collective_id=0, has_side_effects=True, vmem_limit_bytes=63 * 1024 * 1024
        ),
    )(
        adjoint.reshape(block),
        direct.reshape(block),
        cell_weight.reshape(1, cells),
        right_vecs,
        left_vecs,
        inv_root.reshape(1, modes),
    )
    return gram.reshape(near_count * width, width), bal, adj


def solution(mesh):
    in_specs = (
        P("state", "snap"),
        P("state", "snap"),
        P("state"),
        P("snap", None),
        P("snap", None),
        P(),
    )
    out_specs = (P("state", "snap"), P(("state", "snap"), None), P(("state", "snap"), None))
    return jax.shard_map(local, mesh=mesh, in_specs=in_specs, out_specs=out_specs, check_vma=False)
```
